32 devices in a mesh: seq: 2 (over core), fsdp: 16 (over z, y, x).
Axes of the slice: x: 2, y: 2, z: 4, core: 2. Of those that a mesh axis runs over, the one named last changes fastest.
Arguments:
- tokens: bfloat16 [16, 1024, 1024], P('fsdp', 'seq'), may hold values from -6 to 6
- qkv_weight: bfloat16 [1024, 3072], P('fsdp'), may hold values from -0.1875 to 0.1875
- query_bias: bfloat16 [1024], P('fsdp'), may hold values from -1.5 to 1.5
- value_bias: bfloat16 [1024], P('fsdp'), may hold values from -1.5 to 1.5
- proj_weight: bfloat16 [1024, 1024], P('fsdp'), may hold values from -4 to 4
- proj_bias: bfloat16 [1024], P('fsdp'), may hold values from -1.5 to 1.5
- norm1_gain: bfloat16 [1024], P('fsdp'), may hold values from 0.25 to 1.75
- norm1_shift: bfloat16 [1024], P('fsdp'), may hold values from -1.5 to 1.5
- inner_weight: bfloat16 [1024, 4096], P('fsdp'), may hold values from -0.1875 to 0.1875
- inner_bias: bfloat16 [4096], P('fsdp'), may hold values from -2.5 to 2.5
- outer_weight: bfloat16 [4096, 1024], P('fsdp'), may hold values from -0.09375 to 0.09375
- outer_bias: bfloat16 [1024], P('fsdp'), may hold values from -1.5 to 1.5
- norm2_gain: bfloat16 [1024], P('fsdp'), may hold values from 0.25 to 1.75
- norm2_shift: bfloat16 [1024], P('fsdp'), may hold values from -1.5 to 1.5
- cotangent: bfloat16 [16, 1024, 1024], P('fsdp', 'seq'), may hold values from -6 to 6
Outputs:
- mixed: bfloat16 [16, 1024, 1024], P('fsdp', 'seq')
- input_grad: bfloat16 [16, 1024, 1024], P('fsdp', 'seq')
- qkv_grad: float32 [1024, 3072], P('fsdp')
- query_bias_grad: float32 [1024], P('fsdp')
- value_bias_grad: float32 [1024], P('fsdp')
- proj_grad: float32 [1024, 1024], P('fsdp')
- proj_bias_grad: float32 [1024], P('fsdp')
- norm1_gain_grad: float32 [1024], P('fsdp')
- norm1_shift_grad: float32 [1024], P('fsdp')
- inner_grad: float32 [1024, 4096], P('fsdp')
- inner_bias_grad: float32 [4096], P('fsdp')
- outer_grad: float32 [4096, 1024], P('fsdp')
- outer_bias_grad: float32 [1024], P('fsdp')
- norm2_gain_grad: float32 [1024], P('fsdp')
- norm2_shift_grad: float32 [1024], P('fsdp')
The draws below stay inside these ranges and needn't reach their ends.
All inputs are finite; a program needn't handle non-finite values.
Results may differ from the reference program's by a relative error of at most 0.022.
Values may be sent and summed in bfloat16 or wider, within the bound.
A program may use at most 192 MiB of HBM per device.

```python
from functools import partial
import jax
import jax.numpy as jnp
from jax import lax

D = 1024
HEADS = 16
HEAD_DIM = 64
FF = 4096
LENGTH = 1024
SEQS = 16


def block_levels(stream_key, shape, cuts, low, top_value):
    def one(dim, shards_of):
        draws = jax.random.uniform(jax.random.fold_in(jax.random.fold_in(stream_key, 6), dim), (shards_of,), jnp.float32, low / len(cuts), top_value / len(cuts))
        return jnp.repeat(jnp.exp(draws), shape[dim] // shards_of).reshape((-1,) + (1,) * (len(shape) - dim - 1))

    factor_of = one(*cuts[0])
    for cut in cuts[1:]:
        factor_of = factor_of * one(*cut)
    return factor_of


def centred(own_key, shape, width, limit, shards=(), dtype=jnp.bfloat16):
    values = jax.random.normal(own_key, shape, jnp.float32) * width
    if len(shards) > 0:
        values = block_levels(own_key, shape, shards, -0.22, 0.18) * values
    return jnp.clip(values, min=-limit, max=limit).astype(dtype)


def setup_inputs(seed: int = 0) -> dict:
    key_list = jax.random.split(jax.random.key(seed), 16)
    return {
        "tokens": centred(key_list[0], (SEQS, LENGTH, D), 1.0, 6.0, ((0, 16), (1, 2))),
        "qkv_weight": centred(key_list[1], (D, 3 * D), D ** -0.5, 0.1875, ((0, 16),)),
        "query_bias": centred(key_list[2], (D,), 0.3, 1.5, ((0, 16),)),
        "value_bias": centred(key_list[3], (D,), 0.3, 1.5, ((0, 16),)),
        "proj_weight": centred(key_list[4], (D, D), (max(1, 2 * D // LENGTH)) ** -0.5, 4.0, ((0, 16),)),
        "proj_bias": centred(key_list[5], (D,), 0.3, 1.5, ((0, 16),)),
        "norm1_gain": jnp.clip(1.0 + 0.15 * jax.random.normal(key_list[6], (D,), jnp.float32), 0.25, 1.75).astype(jnp.bfloat16),
        "norm1_shift": centred(key_list[7], (D,), 0.3, 1.5, ((0, 16),)),
        "inner_weight": centred(key_list[8], (D, FF), D ** -0.5, 0.1875, ((0, 16),)),
        "inner_bias": centred(key_list[9], (FF,), 0.5, 2.5, ((0, 16),)),
        "outer_weight": centred(key_list[10], (FF, D), FF ** -0.5, 0.09375, ((0, 16),)),
        "outer_bias": centred(key_list[11], (D,), 0.3, 1.5, ((0, 16),)),
        "norm2_gain": jnp.clip(1.0 + 0.15 * jax.random.normal(key_list[12], (D,), jnp.float32), 0.25, 1.75).astype(jnp.bfloat16),
        "norm2_shift": centred(key_list[13], (D,), 0.3, 1.5, ((0, 16),)),
        "cotangent": centred(key_list[14], (SEQS, LENGTH, D), 1.0, 6.0, ((0, 16), (1, 2))),
    }


EPSILON = 1e-12

@jax.custom_vjp
def low(v):
    return lax.optimization_barrier(v.astype(jnp.bfloat16)).astype(jnp.float32)

@jax.custom_vjp
def low_back(v):
    return v

def low_keep(v):
    return (low(v), None)

def low_pass(kept, grad):
    return (grad,)

def back_keep(v):
    return (v, None)

def back_low(kept, grad):
    return (low(grad),)
low.defvjp(low_keep, low_pass)
low_back.defvjp(back_keep, back_low)

def matmul(left_side, right_side):
    return jnp.dot(left_side, right_side, precision=lax.Precision.HIGHEST)

def layer_norm(values, gains, shifts):
    center = values - lax.optimization_barrier(jnp.mean(values, axis=-1, keepdims=True))
    spread = lax.optimization_barrier(jnp.mean(center * center, axis=-1, keepdims=True))
    return center * lax.rsqrt(spread + EPSILON) * gains + shifts

def one_head(triple):
    queries, key_rows, value_rows = triple
    scores = low_back(matmul(queries, key_rows.T) * HEAD_DIM ** (-0.5))
    weights = jax.nn.softmax(scores, axis=-1)
    return matmul(low(weights), value_rows)

def split_heads(tensor):
    return tensor.reshape(LENGTH, HEADS, HEAD_DIM).transpose(1, 0, 2)

def one_sequence(params, inputs):
    qkv_weight, query_bias, value_bias, proj_weight, proj_bias, norm1_gain, norm1_shift, inner_weight, inner_bias, outer_weight, outer_bias, norm2_gain, norm2_shift = params
    joined = matmul(inputs, qkv_weight)
    queries = low(low_back(joined[:, :D] + query_bias))
    key_rows = low(low_back(joined[:, D:2 * D]))
    value_rows = low(low_back(joined[:, 2 * D:] + value_bias))
    per_head = lax.map(jax.checkpoint(one_head), (split_heads(queries), split_heads(key_rows), split_heads(value_rows)))
    context = low(low_back(per_head.transpose(1, 0, 2).reshape(LENGTH, D)))
    attended = low_back(matmul(context, proj_weight) + proj_bias)
    normed_one = layer_norm(inputs + attended, norm1_gain, norm1_shift)
    inner_pre = low_back(matmul(low(normed_one), inner_weight) + inner_bias)
    active = low(jax.nn.gelu(inner_pre, approximate=False))
    branch = low_back(matmul(active, outer_weight) + outer_bias)
    return layer_norm(normed_one + branch, norm2_gain, norm2_shift)

def reference(tokens, qkv_weight, query_bias, value_bias, proj_weight, proj_bias, norm1_gain, norm1_shift, inner_weight, inner_bias, outer_weight, outer_bias, norm2_gain, norm2_shift, cotangent):
    params = tuple((piece.astype(jnp.float32) for piece in (qkv_weight, query_bias, value_bias, proj_weight, proj_bias, norm1_gain, norm1_shift, inner_weight, inner_bias, outer_weight, outer_bias, norm2_gain, norm2_shift)))
    inputs = tokens.astype(jnp.float32)

    def forward(weights, sequences):
        return lax.map(jax.checkpoint(partial(one_sequence, weights)), sequences)
    result, pullback = jax.vjp(forward, params, inputs)
    gradients, input_grad = pullback(cotangent.astype(jnp.float32))
    return (result.astype(jnp.bfloat16), input_grad.astype(jnp.bfloat16), gradients[0], gradients[1], gradients[2], gradients[3], gradients[4], gradients[5], gradients[6], gradients[7], gradients[8], gradients[9], gradients[10], gradients[11], gradients[12])
```

```python
import jax
import jax.numpy as jnp
from jax import lax
from jax.experimental import pallas as pl
from jax.experimental.pallas import tpu as pltpu
from jax.sharding import PartitionSpec as P

HEAD_DIM = 64
EPSILON = 1e-12
F32 = jnp.float32
LOW = jnp.bfloat16


def layer_norm(values, gains, shifts):
    center = values - jnp.mean(values, axis=-1, keepdims=True)
    spread = jnp.mean(center * center, axis=-1, keepdims=True)
    return center * lax.rsqrt(spread + EPSILON) * gains + shifts


def gelu_exact(values):
    return jax.nn.gelu(values, approximate=False)


def fsdp_swap(array, bits):
    count, span = lax.axis_size("seq"), lax.axis_size("fsdp")
    pairs = [
        (s * span + f, s * span + (f ^ bits[s & 1])) for s in range(count) for f in range(span)
    ]
    return lax.ppermute(array, ("seq", "fsdp"), pairs)


def seq_swap(array, bits):
    count = lax.axis_size("seq")
    return lax.ppermute(array, "seq", [(s, s ^ bits) for s in range(count)])


def high_bits():
    bit, bits = lax.axis_size("fsdp") // 2, []
    while bit > 2:
        bits.append(bit)
        bit //= 2
    return bits


def places():
    own = lax.axis_index("fsdp")
    even = lax.axis_index("seq") % 2 == 0
    along_x, along_y = own % 2, own // 2 % 2
    return own, even, along_x, along_y


def gather_seq(part):
    mine, bit = lax.axis_index("seq"), 1
    while bit < lax.axis_size("seq"):
        other = seq_swap(part, bit)
        first = mine // bit % 2 == 0
        part = jnp.concatenate(
            [jnp.where(first, part, other), jnp.where(first, other, part)], axis=1
        )
        bit *= 2
    return part


def gather_weight(shard):
    own, even, along_x, along_y = places()
    width = shard.shape[1] // lax.axis_size("seq")
    held = lax.dynamic_slice_in_dim(shard, lax.axis_index("seq") * width, width, 1)[None]
    rows = shard.shape[0]
    for bit in high_bits():
        other = fsdp_swap(held, (bit, bit))
        first = own // bit % 2 == 0
        held = jnp.stack(
            [jnp.where(first, held, other), jnp.where(first, other, held)], axis=1
        ).reshape(-1, rows, width)
    other = fsdp_swap(held, (1, 2))
    first = jnp.where(even, along_x, along_y) == 0
    held = jnp.stack([jnp.where(first, held, other), jnp.where(first, other, held)], axis=1)
    other = fsdp_swap(held, (2, 1))
    first = jnp.where(even, along_y, along_x) == 0
    near, far = jnp.where(first, held, other), jnp.where(first, other, held)
    whole = jnp.stack(
        [
            near[:, 0],
            jnp.where(even, near[:, 1], far[:, 0]),
            jnp.where(even, far[:, 0], near[:, 1]),
            far[:, 1],
        ],
        axis=1,
    )
    return gather_seq(whole.reshape(-1, width))


def add_swapped(keep, send, bits):
    return keep.astype(F32) + fsdp_swap(send.astype(LOW), bits).astype(F32)


def pick(array, index, axis):
    return lax.dynamic_index_in_dim(array, index, axis, keepdims=False)


def scatter_product(left, right):
    own, even, along_x, along_y = places()
    mine, bit = lax.axis_index("seq"), lax.axis_size("seq") // 2
    half = right.shape[1] // 2
    upper = mine // bit % 2

    def product(start):
        columns = lax.dynamic_slice_in_dim(right, start, half, 1)
        return lax.dot_general(
            left, columns, (((0,), (0,)), ((), ())), preferred_element_type=F32
        )

    arrived = seq_swap(product((1 - upper) * half).astype(LOW), bit)
    total = product(upper * half) + arrived.astype(F32)
    while bit > 1:
        bit //= 2
        half //= 2
        upper = mine // bit % 2
        keep = lax.dynamic_slice_in_dim(total, upper * half, half, 1)
        send = lax.dynamic_slice_in_dim(total, (1 - upper) * half, half, 1)
        total = keep + seq_swap(send.astype(LOW), bit).astype(F32)
    span = lax.axis_size("fsdp")
    rows = total.shape[0] // span
    total = total.astype(LOW).reshape(span // 4, 4, rows, half)
    keep = [jnp.where(even, along_y * 2 + k, k * 2 + along_x) for k in (0, 1)]
    send = [jnp.where(even, (1 - along_y) * 2 + k, k * 2 + 1 - along_x) for k in (0, 1)]
    total = add_swapped(
        jnp.stack([pick(total, place, 1) for place in keep], axis=1),
        jnp.stack([pick(total, place, 1) for place in send], axis=1),
        (2, 1),
    ).astype(LOW)
    here = jnp.where(even, along_x, along_y)
    total = add_swapped(pick(total, here, 1), pick(total, 1 - here, 1), (1, 2))
    for bit in reversed(high_bits()):
        total = total.astype(LOW).reshape(-1, 2, rows, half)
        here = own // bit % 2
        total = add_swapped(pick(total, here, 1), pick(total, 1 - here, 1), (bit, bit))
    return gather_seq(total.reshape(rows, half).astype(LOW)).astype(F32)


def gather_vectors(vectors):
    own = lax.axis_index("fsdp")
    held = jnp.concatenate(vectors)[None]
    bit = lax.axis_size("fsdp") // 2
    while bit >= 1:
        other = fsdp_swap(held, (bit, bit))
        first = own // bit % 2 == 0
        held = jnp.stack(
            [jnp.where(first, held, other), jnp.where(first, other, held)], axis=1
        ).reshape(-1, held.shape[1])
        bit //= 2
    whole, start = [], 0
    for vector in vectors:
        size = vector.shape[0]
        whole.append(held[:, start : start + size].reshape(-1))
        start += size
    return whole


def scatter_vectors(vectors):
    own, span = lax.axis_index("fsdp"), lax.axis_size("fsdp")
    total = jnp.concatenate([vector.reshape(span, -1) for vector in vectors], axis=1)
    bit = 1
    while bit < lax.axis_size("seq"):
        total = total + seq_swap(total, bit)
        bit *= 2
    bit = span // 2
    while bit >= 1:
        total = total.reshape(2, -1, total.shape[-1])
        here = own // bit % 2
        total = pick(total, here, 0) + fsdp_swap(pick(total, 1 - here, 0), (bit, bit))
        bit //= 2
    total, shares, start = total.reshape(-1), [], 0
    for vector in vectors:
        size = vector.shape[0] // span
        shares.append(total[start : start + size])
        start += size
    return shares


def product_of(left, right, left_dim, right_dim):
    return lax.dot_general(
        left, right, (((left_dim,), (right_dim,)), ((), ())), preferred_element_type=F32
    )


def attend_kernel(query_ref, key_ref, value_ref, context_ref, log_ref):
    factor = HEAD_DIM ** (-0.5)
    for head in range(128 // HEAD_DIM):
        lanes = slice(head * HEAD_DIM, (head + 1) * HEAD_DIM)
        scores = product_of(query_ref[:, lanes], key_ref[:, lanes], 1, 1) * factor
        top = jnp.max(scores, axis=1, keepdims=True)
        raised = jnp.exp(scores - top)
        total = jnp.sum(raised, axis=1, keepdims=True)
        summed = product_of(raised.astype(LOW), value_ref[:, lanes], 1, 0)
        context_ref[:, lanes] = summed / total
        log_ref[:, lanes] = jnp.broadcast_to(top + jnp.log(total), summed.shape)


def attend_back_kernel(
    query_ref, key_ref, value_ref, grad_ref, context_ref, log_ref, dq_ref, dk_ref, dv_ref
):
    factor = HEAD_DIM ** (-0.5)
    for head in range(128 // HEAD_DIM):
        lanes = slice(head * HEAD_DIM, (head + 1) * HEAD_DIM)
        queries, keys, values = query_ref[:, lanes], key_ref[:, lanes], value_ref[:, lanes]
        grads = grad_ref[:, lanes]
        delta = jnp.sum(grads.astype(F32) * context_ref[:, lanes], axis=1, keepdims=True)
        log_total = log_ref[:, head * HEAD_DIM : head * HEAD_DIM + 1]
        probs = jnp.exp(product_of(queries, keys, 1, 1) * factor - log_total)
        prob_grad = product_of(grads, values, 1, 1)
        score_grad = (probs * (prob_grad - delta)).astype(LOW)
        dv_ref[:, lanes] = product_of(probs.astype(LOW), grads, 0, 0).astype(LOW)
        dq_ref[:, lanes] = (product_of(score_grad, keys, 1, 0) * factor).astype(LOW)
        dk_ref[:, lanes] = (product_of(score_grad, queries, 0, 0) * factor).astype(LOW)


def attention_call(kernel, dots, row_inputs, pair_rows, out_shape):
    seqs, rows, width = row_inputs[0].shape
    length = pair_rows.shape[1]
    steps = width // 128

    def block(size, shift):
        return pl.BlockSpec((None, size, 128), lambda s, h: (s, 0, h + shift))

    in_specs = [block(rows, 0), block(length, 0), block(length, steps)]
    in_specs += [block(rows, 0)] * (len(row_inputs) - 1)
    return pl.pallas_call(
        kernel,
        grid=(seqs, steps),
        in_specs=in_specs,
        out_specs=[block(shape.shape[1], 0) for shape in out_shape],
        out_shape=out_shape,
        compiler_params=pltpu.CompilerParams(vmem_limit_bytes=40 * 1024 * 1024),
        cost_estimate=pl.CostEstimate(
            flops=8 * dots * seqs * rows * length * width,
            bytes_accessed=4 * seqs * (rows + length) * width * 2,
            transcendentals=seqs * rows * length * width // HEAD_DIM,
        ),
    )(row_inputs[0], pair_rows, pair_rows, *row_inputs[1:])


def on_device(
    tokens,
    qkv_weight,
    query_bias,
    value_bias,
    proj_weight,
    proj_bias,
    norm1_gain,
    norm1_shift,
    inner_weight,
    inner_bias,
    outer_weight,
    outer_bias,
    norm2_gain,
    norm2_shift,
    cotangent,
):
    seq_count, token_rows, width = tokens.shape
    all_rows = seq_count * token_rows
    members = lax.axis_size("seq")
    inputs = tokens.reshape(all_rows, width)
    mix_all = gather_weight(qkv_weight)
    (
        query_shift,
        value_shift,
        proj_shift,
        gain_one,
        shift_one,
        inner_shift,
        outer_shift,
        gain_two,
        shift_two,
    ) = gather_vectors(
        [
            query_bias,
            value_bias,
            proj_bias,
            norm1_gain,
            norm1_shift,
            inner_bias,
            outer_bias,
            norm2_gain,
            norm2_shift,
        ]
    )
    proj_all = gather_weight(proj_weight)
    inner_all = gather_weight(inner_weight)
    outer_all = gather_weight(outer_weight)
    gain_one, shift_one = gain_one.astype(F32), shift_one.astype(F32)
    gain_two, shift_two = gain_two.astype(F32), shift_two.astype(F32)
    joined_shift = jnp.concatenate([query_shift, jnp.zeros_like(query_shift), value_shift])
    joined = (jnp.dot(inputs, mix_all, preferred_element_type=F32) + joined_shift).astype(LOW)
    queries = joined[:, :width].reshape(seq_count, token_rows, width)
    own_pairs = joined[:, width:].reshape(seq_count, token_rows, 2 * width)
    pairs = jnp.concatenate(
        [own_pairs] + [seq_swap(own_pairs, j) for j in range(1, members)], axis=1
    )
    length = token_rows * members
    rows_f32 = jax.ShapeDtypeStruct((seq_count, token_rows, width), F32)
    context, log_total = attention_call(attend_kernel, 2, [queries], pairs, [rows_f32, rows_f32])
    context_low = context.astype(LOW).reshape(all_rows, width)
    attended = jnp.dot(context_low, proj_all, preferred_element_type=F32) + proj_shift
    normed_one, first_pull = jax.vjp(
        layer_norm, inputs.astype(F32) + attended, gain_one, shift_one
    )
    normed_low = normed_one.astype(LOW)
    inner_pre = jnp.dot(normed_low, inner_all, preferred_element_type=F32) + inner_shift
    active, gelu_pull = jax.vjp(gelu_exact, inner_pre)
    active_low = active.astype(LOW)
    branch = jnp.dot(active_low, outer_all, preferred_element_type=F32) + outer_shift
    result, second_pull = jax.vjp(layer_norm, normed_one + branch, gain_two, shift_two)
    upstream = cotangent.reshape(all_rows, width).astype(F32)
    grad_two, grad_gain_two, grad_shift_two = second_pull(upstream)
    grad_two_low = grad_two.astype(LOW)
    grad_outer_shift = jnp.sum(grad_two_low.astype(F32), axis=0)
    grad_outer = scatter_product(active_low, grad_two_low)
    grad_active = lax.dot_general(
        grad_two_low, outer_all, (((1,), (1,)), ((), ())), preferred_element_type=F32
    )
    (grad_inner_pre,) = gelu_pull(grad_active)
    inner_low = grad_inner_pre.astype(LOW)
    grad_inner_shift = jnp.sum(inner_low.astype(F32), axis=0)
    grad_inner = scatter_product(normed_low, inner_low)
    grad_first = grad_two + jnp.dot(inner_low, inner_all.T, preferred_element_type=F32)
    grad_one, grad_gain_one, grad_shift_one = first_pull(grad_first)
    grad_one_low = grad_one.astype(LOW)
    grad_proj_shift = jnp.sum(grad_one_low.astype(F32), axis=0)
    grad_proj = scatter_product(context_low, grad_one_low)
    grad_context = jnp.dot(grad_one_low, proj_all.T, preferred_element_type=F32).astype(LOW)
    pair_out = jax.ShapeDtypeStruct((seq_count, length, width), LOW)
    query_low, key_sums, value_sums = attention_call(
        attend_back_kernel,
        5,
        [queries, grad_context.reshape(seq_count, token_rows, width), context, log_total],
        pairs,
        [jax.ShapeDtypeStruct((seq_count, token_rows, width), LOW), pair_out, pair_out],
    )
    query_low = query_low.reshape(all_rows, width)

    def to_owner(sums):
        total = sums[:, :token_rows].astype(F32)
        for j in range(1, members):
            block = sums[:, j * token_rows : (j + 1) * token_rows]
            total = total + seq_swap(block, j).astype(F32)
        return total.astype(LOW).reshape(all_rows, width)

    key_low, value_low = to_owner(key_sums), to_owner(value_sums)
    joined_grad = jnp.concatenate([query_low, key_low, value_low], axis=1)
    grad_mix = scatter_product(inputs, joined_grad)
    grad_query_shift = jnp.sum(query_low.astype(F32), axis=0)
    grad_value_shift = jnp.sum(value_low.astype(F32), axis=0)
    input_grad = (
        grad_one + jnp.dot(joined_grad, mix_all.T, preferred_element_type=F32)
    ).astype(LOW)
    (
        grad_query_shift,
        grad_value_shift,
        grad_proj_shift,
        grad_gain_one,
        grad_shift_one,
        grad_inner_shift,
        grad_outer_shift,
        grad_gain_two,
        grad_shift_two,
    ) = scatter_vectors(
        [
            grad_query_shift,
            grad_value_shift,
            grad_proj_shift,
            grad_gain_one,
            grad_shift_one,
            grad_inner_shift,
            grad_outer_shift,
            grad_gain_two,
            grad_shift_two,
        ]
    )
    return (
        result.astype(LOW).reshape(tokens.shape),
        input_grad.reshape(tokens.shape),
        grad_mix,
        grad_query_shift,
        grad_value_shift,
        grad_proj,
        grad_proj_shift,
        grad_gain_one,
        grad_shift_one,
        grad_inner,
        grad_inner_shift,
        grad_outer,
        grad_outer_shift,
        grad_gain_two,
        grad_shift_two,
    )


def solution(mesh):
    in_specs = (
        P("fsdp", "seq", None),
        P("fsdp", None),
        P("fsdp"),
        P("fsdp"),
        P("fsdp", None),
        P("fsdp"),
        P("fsdp"),
        P("fsdp"),
        P("fsdp", None),
        P("fsdp"),
        P("fsdp", None),
        P("fsdp"),
        P("fsdp"),
        P("fsdp"),
        P("fsdp", "seq", None),
    )
    out_specs = (
        P("fsdp", "seq", None),
        P("fsdp", "seq", None),
        P("fsdp", None),
        P("fsdp"),
        P("fsdp"),
        P("fsdp", None),
        P("fsdp"),
        P("fsdp"),
        P("fsdp"),
        P("fsdp", None),
        P("fsdp"),
        P("fsdp", None),
        P("fsdp"),
        P("fsdp"),
        P("fsdp"),
    )
    return jax.shard_map(
        on_device, mesh=mesh, in_specs=in_specs, out_specs=out_specs, check_vma=False
    )
```

```python
import jax
import jax.numpy as jnp
from jax import lax
from jax.experimental import pallas as pl
from jax.experimental.pallas import tpu as pltpu
from jax.sharding import PartitionSpec as P

HEAD_DIM = 64
EPSILON = 1e-12
F32 = jnp.float32
LOW = jnp.bfloat16


def layer_norm(values, gains, shifts):
    center = values - jnp.mean(values, axis=-1, keepdims=True)
    spread = jnp.mean(center * center, axis=-1, keepdims=True)
    return center * lax.rsqrt(spread + EPSILON) * gains + shifts


def gelu_exact(values):
    return jax.nn.gelu(values, approximate=False)


def fsdp_swap(array, bits):
    count, span = lax.axis_size("seq"), lax.axis_size("fsdp")
    pairs = [
        (s * span + f, s * span + (f ^ bits[s & 1])) for s in range(count) for f in range(span)
    ]
    return lax.ppermute(array, ("seq", "fsdp"), pairs)


def seq_swap(array, bits):
    count = lax.axis_size("seq")
    return lax.ppermute(array, "seq", [(s, s ^ bits) for s in range(count)])


def high_bits():
    bit, bits = lax.axis_size("fsdp") // 2, []
    while bit > 2:
        bits.append(bit)
        bit //= 2
    return bits


def places():
    own = lax.axis_index("fsdp")
    even = lax.axis_index("seq") % 2 == 0
    along_x, along_y = own % 2, own // 2 % 2
    return own, even, along_x, along_y


def gather_seq(part):
    mine, bit = lax.axis_index("seq"), 1
    while bit < lax.axis_size("seq"):
        other = seq_swap(part, bit)
        first = mine // bit % 2 == 0
        part = jnp.concatenate(
            [jnp.where(first, part, other), jnp.where(first, other, part)], axis=1
        )
        bit *= 2
    return part


def after(array, earlier):
    return lax.optimization_barrier((array, earlier))[0]


def gather_weight(shard, earlier=None):
    own, even, along_x, along_y = places()
    width = shard.shape[1] // lax.axis_size("seq")
    held = lax.dynamic_slice_in_dim(shard, lax.axis_index("seq") * width, width, 1)[None]
    rows = shard.shape[0]
    for bit in high_bits():
        other = fsdp_swap(held, (bit, bit))
        first = own // bit % 2 == 0
        held = jnp.stack(
            [jnp.where(first, held, other), jnp.where(first, other, held)], axis=1
        ).reshape(-1, rows, width)
    other = fsdp_swap(held, (1, 2))
    first = jnp.where(even, along_x, along_y) == 0
    held = jnp.stack([jnp.where(first, held, other), jnp.where(first, other, held)], axis=1)
    if earlier is not None:
        held = after(held, earlier)
    other = fsdp_swap(held, (2, 1))
    first = jnp.where(even, along_y, along_x) == 0
    near, far = jnp.where(first, held, other), jnp.where(first, other, held)
    whole = jnp.stack(
        [
            near[:, 0],
            jnp.where(even, near[:, 1], far[:, 0]),
            jnp.where(even, far[:, 0], near[:, 1]),
            far[:, 1],
        ],
        axis=1,
    )
    return gather_seq(whole.reshape(-1, width))


def add_swapped(keep, send, bits):
    return keep.astype(F32) + fsdp_swap(send.astype(LOW), bits).astype(F32)


def pick(array, index, axis):
    return lax.dynamic_index_in_dim(array, index, axis, keepdims=False)


def scatter_parts(left, right):
    own, even, along_x, along_y = places()
    mine, bit = lax.axis_index("seq"), lax.axis_size("seq") // 2
    half = right.shape[1] // 2
    upper = mine // bit % 2

    def product(start):
        columns = lax.dynamic_slice_in_dim(right, start, half, 1)
        return lax.dot_general(
            left, columns, (((0,), (0,)), ((), ())), preferred_element_type=F32
        )

    arrived = seq_swap((yield product((1 - upper) * half).astype(LOW)), bit)
    total = product(upper * half) + arrived.astype(F32)
    while bit > 1:
        bit //= 2
        half //= 2
        upper = mine // bit % 2
        keep = lax.dynamic_slice_in_dim(total, upper * half, half, 1)
        send = lax.dynamic_slice_in_dim(total, (1 - upper) * half, half, 1)
        total = keep + seq_swap(send.astype(LOW), bit).astype(F32)
    span = lax.axis_size("fsdp")
    rows = total.shape[0] // span
    total = total.astype(LOW).reshape(span // 4, 4, rows, half)
    keep = [jnp.where(even, along_y * 2 + k, k * 2 + along_x) for k in (0, 1)]
    send = [jnp.where(even, (1 - along_y) * 2 + k, k * 2 + 1 - along_x) for k in (0, 1)]
    leaving = yield jnp.stack([pick(total, place, 1) for place in send], axis=1)
    total = add_swapped(
        jnp.stack([pick(total, place, 1) for place in keep], axis=1), leaving, (2, 1)
    ).astype(LOW)
    here = jnp.where(even, along_x, along_y)
    total = add_swapped(pick(total, here, 1), pick(total, 1 - here, 1), (1, 2))
    for bit in reversed(high_bits()):
        total = total.astype(LOW).reshape(-1, 2, rows, half)
        here = own // bit % 2
        total = add_swapped(pick(total, here, 1), pick(total, 1 - here, 1), (bit, bit))
    yield gather_seq(total.reshape(rows, half).astype(LOW)).astype(F32)


def gather_vectors(vectors):
    own = lax.axis_index("fsdp")
    held = jnp.concatenate(vectors)[None]
    bit = lax.axis_size("fsdp") // 2
    while bit >= 1:
        other = fsdp_swap(held, (bit, bit))
        first = own // bit % 2 == 0
        held = jnp.stack(
            [jnp.where(first, held, other), jnp.where(first, other, held)], axis=1
        ).reshape(-1, held.shape[1])
        bit //= 2
    whole, start = [], 0
    for vector in vectors:
        size = vector.shape[0]
        whole.append(held[:, start : start + size].reshape(-1))
        start += size
    return whole


def scatter_vectors(vectors):
    own, span = lax.axis_index("fsdp"), lax.axis_size("fsdp")
    total = jnp.concatenate([vector.reshape(span, -1) for vector in vectors], axis=1)
    bit = 1
    while bit < lax.axis_size("seq"):
        total = total + seq_swap(total, bit)
        bit *= 2
    bit = span // 2
    while bit >= 1:
        total = total.reshape(2, -1, total.shape[-1])
        here = own // bit % 2
        total = pick(total, here, 0) + fsdp_swap(pick(total, 1 - here, 0), (bit, bit))
        bit //= 2
    total, shares, start = total.reshape(-1), [], 0
    for vector in vectors:
        size = vector.shape[0] // span
        shares.append(total[start : start + size])
        start += size
    return shares


def product_of(left, right, left_dim, right_dim):
    return lax.dot_general(
        left, right, (((left_dim,), (right_dim,)), ((), ())), preferred_element_type=F32
    )


def attend_kernel(query_ref, key_ref, value_ref, context_ref, log_ref):
    factor = HEAD_DIM ** (-0.5)
    for head in range(128 // HEAD_DIM):
        lanes = slice(head * HEAD_DIM, (head + 1) * HEAD_DIM)
        scores = product_of(query_ref[:, lanes], key_ref[:, lanes], 1, 1) * factor
        top = jnp.max(scores, axis=1, keepdims=True)
        raised = jnp.exp(scores - top)
        total = jnp.sum(raised, axis=1, keepdims=True)
        summed = product_of(raised.astype(LOW), value_ref[:, lanes], 1, 0)
        context_ref[:, lanes] = summed / total
        log_ref[:, lanes] = jnp.broadcast_to(top + jnp.log(total), summed.shape)


def attend_back_kernel(
    query_ref, key_ref, value_ref, grad_ref, context_ref, log_ref, dq_ref, dk_ref, dv_ref
):
    factor = HEAD_DIM ** (-0.5)
    for head in range(128 // HEAD_DIM):
        lanes = slice(head * HEAD_DIM, (head + 1) * HEAD_DIM)
        queries, keys, values = query_ref[:, lanes], key_ref[:, lanes], value_ref[:, lanes]
        grads = grad_ref[:, lanes]
        delta = jnp.sum(grads.astype(F32) * context_ref[:, lanes], axis=1, keepdims=True)
        log_total = log_ref[:, head * HEAD_DIM : head * HEAD_DIM + 1]
        probs = jnp.exp(product_of(queries, keys, 1, 1) * factor - log_total)
        prob_grad = product_of(grads, values, 1, 1)
        score_grad = (probs * (prob_grad - delta)).astype(LOW)
        dv_ref[:, lanes] = product_of(probs.astype(LOW), grads, 0, 0).astype(LOW)
        dq_ref[:, lanes] = (product_of(score_grad, keys, 1, 0) * factor).astype(LOW)
        dk_ref[:, lanes] = (product_of(score_grad, queries, 0, 0) * factor).astype(LOW)


def attention_call(kernel, dots, row_inputs, pair_rows, out_shape):
    seqs, rows, width = row_inputs[0].shape
    length = pair_rows.shape[1]
    steps = width // 128

    def block(size, shift):
        return pl.BlockSpec((None, size, 128), lambda s, h: (s, 0, h + shift))

    in_specs = [block(rows, 0), block(length, 0), block(length, steps)]
    in_specs += [block(rows, 0)] * (len(row_inputs) - 1)
    return pl.pallas_call(
        kernel,
        grid=(seqs, steps),
        in_specs=in_specs,
        out_specs=[block(shape.shape[1], 0) for shape in out_shape],
        out_shape=out_shape,
        compiler_params=pltpu.CompilerParams(vmem_limit_bytes=40 * 1024 * 1024),
        cost_estimate=pl.CostEstimate(
            flops=8 * dots * seqs * rows * length * width,
            bytes_accessed=4 * seqs * (rows + length) * width * 2,
            transcendentals=seqs * rows * length * width // HEAD_DIM,
        ),
    )(row_inputs[0], pair_rows, pair_rows, *row_inputs[1:])


def on_device(
    tokens,
    qkv_weight,
    query_bias,
    value_bias,
    proj_weight,
    proj_bias,
    norm1_gain,
    norm1_shift,
    inner_weight,
    inner_bias,
    outer_weight,
    outer_bias,
    norm2_gain,
    norm2_shift,
    cotangent,
):
    seq_count, token_rows, width = tokens.shape
    all_rows = seq_count * token_rows
    members = lax.axis_size("seq")
    inputs = tokens.reshape(all_rows, width)
    mix_all = gather_weight(qkv_weight)
    (
        query_shift,
        value_shift,
        proj_shift,
        gain_one,
        shift_one,
        inner_shift,
        outer_shift,
        gain_two,
        shift_two,
    ) = gather_vectors(
        [
            query_bias,
            value_bias,
            proj_bias,
            norm1_gain,
            norm1_shift,
            inner_bias,
            outer_bias,
            norm2_gain,
            norm2_shift,
        ]
    )
    proj_all = gather_weight(proj_weight)
    gain_one, shift_one = gain_one.astype(F32), shift_one.astype(F32)
    gain_two, shift_two = gain_two.astype(F32), shift_two.astype(F32)
    joined_shift = jnp.concatenate([query_shift, jnp.zeros_like(query_shift), value_shift])
    joined = (jnp.dot(inputs, mix_all, preferred_element_type=F32) + joined_shift).astype(LOW)
    inner_all = gather_weight(inner_weight, joined)
    queries = joined[:, :width].reshape(seq_count, token_rows, width)
    own_pairs = joined[:, width:].reshape(seq_count, token_rows, 2 * width)
    pairs = jnp.concatenate(
        [own_pairs] + [seq_swap(own_pairs, j) for j in range(1, members)], axis=1
    )
    length = token_rows * members
    rows_f32 = jax.ShapeDtypeStruct((seq_count, token_rows, width), F32)
    context, log_total = attention_call(attend_kernel, 2, [queries], pairs, [rows_f32, rows_f32])
    outer_all = gather_weight(outer_weight, context)
    context_low = context.astype(LOW).reshape(all_rows, width)
    attended = jnp.dot(context_low, proj_all, preferred_element_type=F32) + proj_shift
    normed_one, first_pull = jax.vjp(
        layer_norm, inputs.astype(F32) + attended, gain_one, shift_one
    )
    normed_low = normed_one.astype(LOW)
    inner_pre = jnp.dot(normed_low, inner_all, preferred_element_type=F32) + inner_shift
    active, gelu_pull = jax.vjp(gelu_exact, inner_pre)
    active_low = active.astype(LOW)
    branch = jnp.dot(active_low, outer_all, preferred_element_type=F32) + outer_shift
    result, second_pull = jax.vjp(layer_norm, normed_one + branch, gain_two, shift_two)
    upstream = cotangent.reshape(all_rows, width).astype(F32)
    grad_two, grad_gain_two, grad_shift_two = second_pull(upstream)
    grad_two_low = grad_two.astype(LOW)
    grad_outer_shift = jnp.sum(grad_two_low.astype(F32), axis=0)
    outer_parts = scatter_parts(active_low, grad_two_low)
    outer_sent, grad_two_low = lax.optimization_barrier((next(outer_parts), grad_two_low))
    grad_active = lax.dot_general(
        grad_two_low, outer_all, (((1,), (1,)), ((), ())), preferred_element_type=F32
    )
    (grad_inner_pre,) = gelu_pull(grad_active)
    inner_low = grad_inner_pre.astype(LOW)
    grad_inner_shift = jnp.sum(inner_low.astype(F32), axis=0)
    inner_parts = scatter_parts(normed_low, inner_low)
    outer_sent, inner_sent, inner_low = lax.optimization_barrier(
        (outer_parts.send(outer_sent), next(inner_parts), inner_low)
    )
    grad_first = grad_two + jnp.dot(inner_low, inner_all.T, preferred_element_type=F32)
    grad_one, grad_gain_one, grad_shift_one = first_pull(grad_first)
    grad_one_low = grad_one.astype(LOW)
    grad_proj_shift = jnp.sum(grad_one_low.astype(F32), axis=0)
    proj_parts = scatter_parts(context_low, grad_one_low)
    inner_sent, proj_sent, grad_one_low = lax.optimization_barrier(
        (inner_parts.send(inner_sent), next(proj_parts), grad_one_low)
    )
    grad_outer = outer_parts.send(outer_sent)
    grad_inner = inner_parts.send(inner_sent)
    grad_proj = proj_parts.send(proj_parts.send(proj_sent))
    grad_context = jnp.dot(grad_one_low, proj_all.T, preferred_element_type=F32).astype(LOW)
    pair_out = jax.ShapeDtypeStruct((seq_count, length, width), LOW)
    query_low, key_sums, value_sums = attention_call(
        attend_back_kernel,
        5,
        [queries, grad_context.reshape(seq_count, token_rows, width), context, log_total],
        pairs,
        [jax.ShapeDtypeStruct((seq_count, token_rows, width), LOW), pair_out, pair_out],
    )
    query_low = query_low.reshape(all_rows, width)

    def to_owner(sums):
        total = sums[:, :token_rows].astype(F32)
        for j in range(1, members):
            block = sums[:, j * token_rows : (j + 1) * token_rows]
            total = total + seq_swap(block, j).astype(F32)
        return total.astype(LOW).reshape(all_rows, width)

    key_low, value_low = to_owner(key_sums), to_owner(value_sums)
    joined_grad = jnp.concatenate([query_low, key_low, value_low], axis=1)
    mix_parts = scatter_parts(inputs, joined_grad)
    grad_mix = mix_parts.send(mix_parts.send(next(mix_parts)))
    grad_query_shift = jnp.sum(query_low.astype(F32), axis=0)
    grad_value_shift = jnp.sum(value_low.astype(F32), axis=0)
    input_grad = (
        grad_one + jnp.dot(joined_grad, mix_all.T, preferred_element_type=F32)
    ).astype(LOW)
    (
        grad_query_shift,
        grad_value_shift,
        grad_proj_shift,
        grad_gain_one,
        grad_shift_one,
        grad_inner_shift,
        grad_outer_shift,
        grad_gain_two,
        grad_shift_two,
    ) = scatter_vectors(
        [
            grad_query_shift,
            grad_value_shift,
            grad_proj_shift,
            grad_gain_one,
            grad_shift_one,
            grad_inner_shift,
            grad_outer_shift,
            grad_gain_two,
            grad_shift_two,
        ]
    )
    return (
        result.astype(LOW).reshape(tokens.shape),
        input_grad.reshape(tokens.shape),
        grad_mix,
        grad_query_shift,
        grad_value_shift,
        grad_proj,
        grad_proj_shift,
        grad_gain_one,
        grad_shift_one,
        grad_inner,
        grad_inner_shift,
        grad_outer,
        grad_outer_shift,
        grad_gain_two,
        grad_shift_two,
    )


def solution(mesh):
    in_specs = (
        P("fsdp", "seq", None),
        P("fsdp", None),
        P("fsdp"),
        P("fsdp"),
        P("fsdp", None),
        P("fsdp"),
        P("fsdp"),
        P("fsdp"),
        P("fsdp", None),
        P("fsdp"),
        P("fsdp", None),
        P("fsdp"),
        P("fsdp"),
        P("fsdp"),
        P("fsdp", "seq", None),
    )
    out_specs = (
        P("fsdp", "seq", None),
        P("fsdp", "seq", None),
        P("fsdp", None),
        P("fsdp"),
        P("fsdp"),
        P("fsdp", None),
        P("fsdp"),
        P("fsdp"),
        P("fsdp"),
        P("fsdp", None),
        P("fsdp"),
        P("fsdp", None),
        P("fsdp"),
        P("fsdp"),
        P("fsdp"),
    )
    return jax.shard_map(
        on_device, mesh=mesh, in_specs=in_specs, out_specs=out_specs, check_vma=False
    )
```
